32 devices in a mesh: dp: 8 (over y, x, core), seq: 4 (over z).
Axes of the slice: x: 2, y: 2, z: 4, core: 2. Of those that a mesh axis runs over, the one named last changes fastest.
Arguments:
- inputs: bfloat16 [3, 8, 1024, 1024], P(None, 'dp', 'seq'), may hold values from -6 to 6
- upstream: bfloat16 [3, 8, 1024, 1024], P(None, 'dp', 'seq'), may hold values from -6 to 6
- norm_gain: float32 [1024], replicated, may hold values from 0.5 to 1.5
- query_weight: bfloat16 [1024, 1024], P('dp', 'seq'), may hold values from -0.1875 to 0.1875
- key_weight: bfloat16 [1024, 1024], P('dp', 'seq'), may hold values from -0.1875 to 0.1875
- value_weight: bfloat16 [1024, 2048], P('dp', 'seq'), may hold values from -0.1875 to 0.1875
- gate_weight: bfloat16 [1024, 2048], P('dp', 'seq'), may hold values from -0.1875 to 0.1875
- rate_weight: bfloat16 [1024, 16], P('dp', 'seq'), may hold values from -0.1875 to 0.1875
- conv_weight: float32 [4, 4096], replicated, may hold values from -2.5 to 2.5
- decay_log: float32 [8], replicated, may hold values from -7 to -2
- decay_bias: float32 [8], replicated, may hold values from -1 to 1
- out_gain: float32 [256], replicated, may hold values from 0.5 to 1.5
- output_weight: bfloat16 [2048, 1024], P('dp', 'seq'), may hold values from -0.125 to 0.125
- ffn_gain: float32 [1024], replicated, may hold values from 0.5 to 1.5
- ffn_gate: bfloat16 [1024, 2816], P('dp', 'seq'), may hold values from -0.1875 to 0.1875
- ffn_up: bfloat16 [1024, 2816], P('dp', 'seq'), may hold values from -0.1875 to 0.1875
- ffn_down: bfloat16 [2816, 1024], P('dp', 'seq'), may hold values from -0.109375 to 0.109375
Outputs:
- outputs: bfloat16 [3, 8, 1024, 1024], P(None, 'dp', 'seq')
- input_grad: float32 [3, 8, 1024, 1024], P(None, 'dp', 'seq')
- norm_gain_grad: float32 [1024], replicated
- query_weight_grad: float32 [1024, 1024], P('dp', 'seq')
- key_weight_grad: float32 [1024, 1024], P('dp', 'seq')
- value_weight_grad: float32 [1024, 2048], P('dp', 'seq')
- gate_weight_grad: float32 [1024, 2048], P('dp', 'seq')
- rate_weight_grad: float32 [1024, 16], P('dp', 'seq')
- conv_weight_grad: float32 [4, 4096], replicated
- decay_log_grad: float32 [8], replicated
- decay_bias_grad: float32 [8], replicated
- out_gain_grad: float32 [256], replicated
- output_weight_grad: float32 [2048, 1024], P('dp', 'seq')
- ffn_gain_grad: float32 [1024], replicated
- ffn_gate_grad: float32 [1024, 2816], P('dp', 'seq')
- ffn_up_grad: float32 [1024, 2816], P('dp', 'seq')
- ffn_down_grad: float32 [2816, 1024], P('dp', 'seq')
The draws below stay inside these ranges and needn't reach their ends.
All inputs are finite; a program needn't handle non-finite values.
Results may differ from the reference program's by a relative error of at most 0.017.
Values may be sent and summed in bfloat16 or wider, within the bound.
A program may use at most 512 MiB of HBM per device.

```python
import jax
import jax.numpy as jnp
from jax import lax

D = 1024
HEADS = 8
DV = 256
FF = 2816
CONV = 4
GROUP = 64
MB = 3
HK = 1024
HV = 2048
LENGTH = 1024
NSEQ = 8


def block_levels(key, extent, split, least, high):
    def one(axis_at, blocks):
        heights = jax.random.uniform(jax.random.fold_in(jax.random.fold_in(key, 6), axis_at), (blocks,), jnp.float32, least / len(split), high / len(split))
        return jnp.repeat(jnp.exp(heights), extent[axis_at] // blocks).reshape((-1,) + (1,) * (len(extent) - axis_at - 1))

    level = one(*split[0])
    for cut in split[1:]:
        level = level * one(*cut)
    return level


def centred(rng, dims, width, bound, pieces=(), held_as=jnp.bfloat16):
    factor_of = block_levels(rng, dims, pieces, -0.22, 0.18) if pieces else 1.0
    values = jax.random.normal(rng, dims, jnp.float32) * width * factor_of
    return jnp.minimum(jnp.maximum(values, -bound), bound).astype(held_as)


def setup_inputs(seed: int = 0) -> dict:
    seeds = jax.random.split(jax.random.key(seed), 18)
    return {
        "inputs": centred(seeds[0], (MB, NSEQ, LENGTH, D), 1.0, 6.0, ((1, 8), (2, 4))),
        "upstream": centred(seeds[1], (MB, NSEQ, LENGTH, D), 1.0, 6.0, ((1, 8), (2, 4))),
        "norm_gain": jnp.clip(1.0 + 0.1 * jax.random.normal(seeds[2], (D,), jnp.float32), 0.5, 1.5),
        "query_weight": centred(seeds[3], (D, HK), D ** -0.5, 0.1875, ((0, 8), (1, 4))),
        "key_weight": centred(seeds[4], (D, HK), D ** -0.5, 0.1875, ((0, 8), (1, 4))),
        "value_weight": centred(seeds[5], (D, HV), D ** -0.5, 0.1875, ((0, 8), (1, 4))),
        "gate_weight": centred(seeds[6], (D, HV), D ** -0.5, 0.1875, ((0, 8), (1, 4))),
        "rate_weight": centred(seeds[7], (D, 2 * HEADS), D ** -0.5, 0.1875, ((0, 8), (1, 4))),
        "conv_weight": centred(seeds[8], (CONV, 2 * HK + HV), 0.5, 2.5, (), jnp.float32),
        "decay_log": jnp.clip(jax.random.uniform(seeds[9], (HEADS,), jnp.float32, -7.0, -2.0), -7.0, -2.0),
        "decay_bias": jnp.clip(jax.random.uniform(seeds[10], (HEADS,), jnp.float32, -1.0, 1.0), -1.0, 1.0),
        "out_gain": jnp.clip(1.0 + 0.1 * jax.random.normal(seeds[11], (DV,), jnp.float32), 0.5, 1.5),
        "output_weight": centred(seeds[12], (HV, D), HV ** -0.5, 0.125, ((0, 8), (1, 4))),
        "ffn_gain": jnp.clip(1.0 + 0.1 * jax.random.normal(seeds[13], (D,), jnp.float32), 0.5, 1.5),
        "ffn_gate": centred(seeds[14], (D, FF), D ** -0.5, 0.1875, ((0, 8), (1, 4))),
        "ffn_up": centred(seeds[15], (D, FF), D ** -0.5, 0.1875, ((0, 8), (1, 4))),
        "ffn_down": centred(seeds[16], (FF, D), FF ** -0.5, 0.109375, ((0, 8), (1, 4))),
    }


EPSILON = 1e-06

@jax.custom_vjp
def low(v):
    return lax.optimization_barrier(v.astype(jnp.bfloat16)).astype(jnp.float32)

@jax.custom_vjp
def low_back(v):
    return v

def low_keep(v):
    return (low(v), None)

def low_pass(kept, grad):
    return (grad,)

def back_keep(v):
    return (v, None)

def back_low(kept, grad):
    return (low(grad),)
low.defvjp(low_keep, low_pass)
low_back.defvjp(back_keep, back_low)

def high_dot(left_mat, right_mat):
    return jnp.dot(left_mat, right_mat, precision=lax.Precision.HIGHEST, preferred_element_type=jnp.float32)

def rms_scale(values, gain_vec):
    return values * lax.rsqrt(lax.optimization_barrier(jnp.mean(values * values, axis=-1, keepdims=True)) + EPSILON) * gain_vec

def swiglu_product(gate_vals, up_vals):
    return jax.nn.silu(gate_vals) * up_vals

def gate_output(mixture, gate_pre, out_gain):
    head_count = mixture.shape[-2]
    gated_rows = rms_scale(mixture, out_gain) * jax.nn.silu(gate_pre.reshape(gate_pre.shape[:-1] + (head_count, -1)))
    return gated_rows.reshape(gate_pre.shape)

def prepare(query_ext, key_ext, value_ext, rate_pre, conv_weight, decay_log, decay_bias):
    conv_lead = conv_weight.shape[0] - 1
    length = query_ext.shape[1] - conv_lead
    head_count = decay_log.shape[0]
    query_width = query_ext.shape[2]
    key_dim = query_width // head_count
    batch_size = query_ext.shape[0]

    def convolve(extended, kernel):
        summed_taps = kernel[0] * extended[:, 0:length]
        for offset_idx in range(1, conv_lead + 1):
            summed_taps = summed_taps + kernel[offset_idx] * extended[:, offset_idx:offset_idx + length]
        return jax.nn.silu(summed_taps)
    queries = convolve(query_ext, conv_weight[:, :query_width]).reshape(batch_size, length, head_count, key_dim)
    key_rows = convolve(key_ext, conv_weight[:, query_width:2 * query_width]).reshape(batch_size, length, head_count, key_dim)
    values = convolve(value_ext, conv_weight[:, 2 * query_width:]).reshape(batch_size, length, head_count, -1)
    queries = queries * lax.rsqrt(lax.optimization_barrier(jnp.sum(queries * queries, axis=-1, keepdims=True)) + EPSILON) * key_dim ** (-0.5)
    key_rows = key_rows * lax.rsqrt(lax.optimization_barrier(jnp.sum(key_rows * key_rows, axis=-1, keepdims=True)) + EPSILON)
    beta_rows = jax.nn.sigmoid(rate_pre[..., head_count:])
    decays = -jnp.exp(decay_log) * jax.nn.softplus(rate_pre[..., :head_count] + decay_bias)
    return (queries, key_rows, values, beta_rows, decays)

def group_terms(queries, key_rows, values, beta_rows, decays):
    group_len = decays.shape[0]
    cumulative = jnp.cumsum(decays)
    row_index = lax.broadcasted_iota(jnp.int32, (group_len, group_len), 0)
    col_index = lax.broadcasted_iota(jnp.int32, (group_len, group_len), 1)
    strict_lower = row_index > col_index
    lower_incl = row_index >= col_index
    decay_ratio = jnp.exp(jnp.where(lower_incl, cumulative[:, None] - cumulative[None, :], 0.0))
    mixing = jnp.where(strict_lower, beta_rows[:, None] * high_dot(key_rows, key_rows.T) * decay_ratio, 0.0)
    identity = jnp.eye(group_len, dtype=jnp.float32)
    inverse = identity - mixing
    powered = mixing
    covered = 2
    while covered < group_len:
        powered = high_dot(powered, powered)
        inverse = high_dot(inverse, identity + powered)
        covered = covered * 2
    solved = inverse * beta_rows[None, :]
    growth = jnp.exp(cumulative)
    wy_keys = high_dot(solved, growth[:, None] * key_rows)
    wy_values = high_dot(solved, values)
    scores = jnp.where(lower_incl, high_dot(queries, key_rows.T) * decay_ratio, 0.0)
    tail_keys = jnp.exp(cumulative[-1] - cumulative)[:, None] * key_rows
    return (growth, wy_keys, wy_values, scores, tail_keys)

def delta_head(queries, key_rows, values, beta_rows, decays):
    group_count = queries.shape[0] // GROUP
    group_data = (queries.reshape(group_count, GROUP, -1), key_rows.reshape(group_count, GROUP, -1), values.reshape(group_count, GROUP, -1), beta_rows.reshape(group_count, GROUP), decays.reshape(group_count, GROUP))

    def group_step(state_mat, group_block):
        group_query, group_keys, group_values, group_betas, group_decays = group_block
        growth, wy_keys, wy_values, scores, tail_keys = group_terms(group_query, group_keys, group_values, group_betas, group_decays)
        fresh_values = wy_values - high_dot(wy_keys, state_mat)
        result = growth[:, None] * high_dot(group_query, state_mat) + high_dot(scores, fresh_values)
        state_mat = growth[-1] * state_mat + high_dot(tail_keys.T, fresh_values)
        return (state_mat, result)
    zero_state = jnp.zeros((queries.shape[1], values.shape[1]), jnp.float32)
    final_state, results = lax.scan(jax.checkpoint(group_step), zero_state, group_data)
    return results.reshape(-1, values.shape[1])

def forward(tokens, params):
    norm_gain, query_weight, key_weight, value_weight, gate_weight, rate_weight, conv_weight, decay_log, decay_bias, out_gain, output_weight, ffn_gain, ffn_gate, ffn_up, ffn_down = params
    normed = low(rms_scale(tokens, norm_gain))
    query_pre = low_back(low(high_dot(normed, query_weight)))
    key_pre = low_back(low(high_dot(normed, key_weight)))
    value_pre = low_back(low(high_dot(normed, value_weight)))
    gate_pre = low_back(high_dot(normed, gate_weight))
    rate_pre = low_back(high_dot(normed, rate_weight))
    conv_lead = conv_weight.shape[0] - 1

    def extend(values):
        return jnp.concatenate([jnp.zeros((conv_lead, values.shape[1]), jnp.float32), values], axis=0)[None]
    queries, key_rows, values, beta_rows, decays = prepare(extend(query_pre), extend(key_pre), extend(value_pre), rate_pre[None], conv_weight, decay_log, decay_bias)
    queries = low_back(low(queries))
    key_rows = low_back(low(key_rows))
    values = low_back(low(values))
    mixture = jax.vmap(delta_head, in_axes=(1, 1, 1, 1, 1), out_axes=1)(queries[0], key_rows[0], values[0], beta_rows[0], decays[0])
    gated_rows = low(gate_output(mixture, gate_pre, out_gain))
    branch = low_back(high_dot(gated_rows, output_weight))
    hidden = tokens + branch
    normed_two = low(rms_scale(hidden, ffn_gain))
    gate_vals = low_back(high_dot(normed_two, ffn_gate))
    up_vals = low_back(high_dot(normed_two, ffn_up))
    product = low(swiglu_product(gate_vals, up_vals))
    return hidden + low_back(high_dot(product, ffn_down))

def reference(inputs, upstream, norm_gain, query_weight, key_weight, value_weight, gate_weight, rate_weight, conv_weight, decay_log, decay_bias, out_gain, output_weight, ffn_gain, ffn_gate, ffn_up, ffn_down):
    params = tuple((argument.astype(jnp.float32) for argument in (norm_gain, query_weight, key_weight, value_weight, gate_weight, rate_weight, conv_weight, decay_log, decay_bias, out_gain, output_weight, ffn_gain, ffn_gate, ffn_up, ffn_down)))
    tokens_all = inputs.astype(jnp.float32).reshape(-1, LENGTH, D)
    grads_all = upstream.astype(jnp.float32).reshape(-1, LENGTH, D)

    def one_sequence(totals, seq_pair):
        tokens, cotangent = seq_pair
        result, backward = jax.vjp(forward, tokens, params)
        token_grad, param_grads = backward(cotangent)
        totals = jax.tree.map(jnp.add, totals, param_grads)
        return (totals, (result.astype(jnp.bfloat16), token_grad))
    zero_grads = jax.tree.map(jnp.zeros_like, params)
    totals, (results, token_grads) = lax.scan(one_sequence, zero_grads, (tokens_all, grads_all))
    return (results.reshape(inputs.shape), token_grads.reshape(inputs.shape), totals[0], totals[1], totals[2], totals[3], totals[4], totals[5], totals[6], totals[7], totals[8], totals[9], totals[10], totals[11], totals[12], totals[13], totals[14])
```

```python
import jax
import jax.numpy as jnp
from jax import lax
from jax.sharding import PartitionSpec as P

GROUP = 64


EPSILON = 1e-06


def passed_along(block, axis, distance):
    devices = range(lax.axis_size(axis))
    route = [(i - distance, i) for i in devices if i - distance in devices]
    return lax.ppermute(block, axis, route)


def plain_dot(left_mat, right_mat):
    return jnp.dot(left_mat, right_mat, preferred_element_type=jnp.float32)


def back_dot(left_mat, right_mat):
    return lax.dot_general(
        left_mat, right_mat, (((1,), (1,)), ((), ())), preferred_element_type=jnp.float32
    )


def weight_dot(left_mat, right_mat):
    return lax.dot_general(
        left_mat, right_mat, (((0,), (0,)), ((), ())), preferred_element_type=jnp.float32
    )


def mid_dot(left_mat, right_mat, formula):
    return jnp.einsum(formula, left_mat, right_mat, precision=lax.Precision.HIGH)


def rms_scale(values, gain_vec):
    return (
        values * lax.rsqrt(jnp.mean(values * values, axis=-1, keepdims=True) + EPSILON) * gain_vec
    )


def swiglu_product(gate_vals, up_vals):
    return jax.nn.silu(gate_vals) * up_vals


def gate_output(mixture, gate_pre, out_gain):
    head_count = mixture.shape[-2]
    gated_rows = rms_scale(mixture, out_gain) * jax.nn.silu(
        gate_pre.reshape(gate_pre.shape[:-1] + (head_count, -1))
    )
    return gated_rows.reshape(gate_pre.shape)


def prepare(query_ext, key_ext, value_ext, rate_pre, conv_weight, decay_log, decay_bias):
    conv_lead = conv_weight.shape[0] - 1
    length = query_ext.shape[1] - conv_lead
    head_count = decay_log.shape[0]
    query_width = query_ext.shape[2]
    key_dim = query_width // head_count
    batch_size = query_ext.shape[0]

    def convolve(extended, kernel):
        summed_taps = kernel[0] * extended[:, 0:length]
        for offset_idx in range(1, conv_lead + 1):
            summed_taps = (
                summed_taps + kernel[offset_idx] * extended[:, offset_idx : offset_idx + length]
            )
        return jax.nn.silu(summed_taps)

    queries = convolve(query_ext, conv_weight[:, :query_width]).reshape(
        batch_size, length, head_count, key_dim
    )
    key_rows = convolve(key_ext, conv_weight[:, query_width : 2 * query_width]).reshape(
        batch_size, length, head_count, key_dim
    )
    values = convolve(value_ext, conv_weight[:, 2 * query_width :]).reshape(
        batch_size, length, head_count, -1
    )
    queries = (
        queries
        * lax.rsqrt(jnp.sum(queries * queries, axis=-1, keepdims=True) + EPSILON)
        * key_dim ** (-0.5)
    )
    key_rows = key_rows * lax.rsqrt(jnp.sum(key_rows * key_rows, axis=-1, keepdims=True) + EPSILON)
    beta_rows = jax.nn.sigmoid(rate_pre[..., head_count:])
    decays = -jnp.exp(decay_log) * jax.nn.softplus(rate_pre[..., :head_count] + decay_bias)
    return (queries, key_rows, values, beta_rows, decays)


@jax.custom_vjp
def unit_inverse(mixing):
    size = mixing.shape[-1]
    row_index = lax.broadcasted_iota(jnp.int32, (size, size), 0)
    col_index = lax.broadcasted_iota(jnp.int32, (size, size), 1)

    def between(width):
        same = row_index // (2 * width) == col_index // (2 * width)
        return same & (row_index // width > col_index // width)

    inverse = jnp.eye(size, dtype=jnp.float32) - jnp.where(between(1), mixing, 0.0)
    width = 2
    while width < size:
        linked = jnp.where(between(width), mixing, 0.0)
        inverse = inverse - mid_dot(
            mid_dot(inverse, linked, "...ij,...jk->...ik"), inverse, "...ij,...jk->...ik"
        )
        width = width * 2
    return inverse


def unit_inverse_keep(mixing):
    inverse = unit_inverse(mixing)
    return inverse, inverse


def unit_inverse_back(inverse, grad):
    partial = mid_dot(inverse, grad, "...ji,...jk->...ik")
    return (-mid_dot(partial, inverse, "...ij,...kj->...ik"),)


unit_inverse.defvjp(unit_inverse_keep, unit_inverse_back)


def group_maps(queries, key_rows, values, beta_rows, decays):
    group_len = decays.shape[-1]
    key_dim = key_rows.shape[-1]
    row_index = lax.broadcasted_iota(jnp.int32, (group_len, group_len), 0)
    col_index = lax.broadcasted_iota(jnp.int32, (group_len, group_len), 1)
    strict_lower = row_index > col_index
    lower_incl = row_index >= col_index
    cumulative = jnp.sum(jnp.where(lower_incl, decays[..., None, :], 0.0), axis=-1)
    decay_ratio = jnp.exp(
        jnp.where(lower_incl, cumulative[..., :, None] - cumulative[..., None, :], 0.0)
    )
    overlaps = jnp.einsum("...ik,...jk->...ij", key_rows, key_rows)
    mixing = jnp.where(strict_lower, beta_rows[..., :, None] * overlaps * decay_ratio, 0.0)
    solved = unit_inverse(mixing) * beta_rows[..., None, :]
    growth = jnp.exp(cumulative)[..., None]
    wy_keys = mid_dot(solved, growth * key_rows, "...ij,...jk->...ik")
    wy_values = mid_dot(solved, values, "...ij,...jk->...ik")
    matches = jnp.einsum("...ik,...jk->...ij", queries, key_rows)
    scores = jnp.where(lower_incl, matches * decay_ratio, 0.0)
    tail_keys = jnp.exp(cumulative[..., -1:] - cumulative)[..., None] * key_rows
    step_map = growth[..., -1:, :] * jnp.eye(key_dim, dtype=jnp.float32) - mid_dot(
        tail_keys, wy_keys, "...tk,...tj->...kj"
    )
    step_offset = mid_dot(tail_keys, wy_values, "...tk,...tv->...kv")
    read_map = growth * queries - mid_dot(scores, wy_keys, "...ij,...jk->...ik")
    read_offset = mid_dot(scores, wy_values, "...ij,...jk->...ik")
    return (step_map, step_offset, read_map, read_offset)


def round_trip(values):
    return values.astype(jnp.bfloat16).astype(jnp.float32)


def gather_block(matrices):
    wide = [0, 1, 2, 3, 4, 6, 7]
    tall = [5, 8]
    wide_all = lax.all_gather(jnp.concatenate([matrices[i] for i in wide], axis=1), "seq")
    tall_all = lax.all_gather(jnp.concatenate([matrices[i] for i in tall], axis=0), "seq")
    rows = {}
    start = 0
    for i in wide:
        stop = start + matrices[i].shape[1]
        rows[i] = wide_all[:, :, start:stop]
        start = stop
    start = 0
    for i in tall:
        stop = start + matrices[i].shape[0]
        rows[i] = tall_all[:, start:stop]
        start = stop
    return tuple(
        lax.all_gather(
            rows[i].transpose(1, 0, 2).reshape(matrices[i].shape[0], -1), "dp", axis=0, tiled=True
        )
        for i in range(len(matrices))
    )


def row_sum(grad):
    return lax.psum_scatter(
        grad.astype(jnp.bfloat16), "dp", scatter_dimension=0, tiled=True
    )


def column_sums(grads):
    wide = [0, 1, 2, 3, 4, 6, 7]
    tall = [5, 8]
    parts = lax.axis_size("seq")
    split = [g.reshape(g.shape[0], parts, -1).transpose(1, 0, 2) for g in grads]
    wide_sum = lax.psum_scatter(
        jnp.concatenate([split[i] for i in wide], axis=2), "seq", scatter_dimension=0
    )
    tall_sum = lax.psum_scatter(
        jnp.concatenate([split[i] for i in tall], axis=1), "seq", scatter_dimension=0
    )
    found = {}
    start = 0
    for i in wide:
        stop = start + split[i].shape[2]
        found[i] = wide_sum[:, start:stop].astype(jnp.float32)
        start = stop
    start = 0
    for i in tall:
        stop = start + split[i].shape[1]
        found[i] = tall_sum[start:stop].astype(jnp.float32)
        start = stop
    return tuple(found[i] for i in range(len(grads)))


def hop_sum(block, axis_distance):
    return passed_along(block.astype(jnp.bfloat16), "seq", axis_distance).astype(jnp.float32)


def shards(
    inputs,
    upstream,
    norm_gain,
    query_weight,
    key_weight,
    value_weight,
    gate_weight,
    rate_weight,
    conv_weight,
    decay_log,
    decay_bias,
    out_gain,
    output_weight,
    ffn_gain,
    ffn_gate,
    ffn_up,
    ffn_down,
):
    batch_count = inputs.shape[0] * inputs.shape[1]
    segment_len = inputs.shape[2]
    model_width = inputs.shape[3]
    row_count = batch_count * segment_len
    conv_lead = conv_weight.shape[0] - 1
    key_width = query_weight.shape[1] * lax.axis_size("seq")
    value_width = value_weight.shape[1] * lax.axis_size("seq")
    tokens = inputs.reshape(row_count, model_width).astype(jnp.float32)
    gathered = gather_block((
        query_weight,
        key_weight,
        value_weight,
        gate_weight,
        rate_weight,
        output_weight,
        ffn_gate,
        ffn_up,
        ffn_down,
    ))
    w_query, w_key, w_value, w_gate, w_rate, w_output, w_ffgate, w_ffup, w_ffdown = gathered
    normed_full, norm_back = jax.vjp(rms_scale, tokens, norm_gain)
    normed = normed_full.astype(jnp.bfloat16)
    query_pre = (
        plain_dot(normed, w_query).astype(jnp.bfloat16).reshape(batch_count, segment_len, key_width)
    )
    key_pre = (
        plain_dot(normed, w_key).astype(jnp.bfloat16).reshape(batch_count, segment_len, key_width)
    )
    value_pre = (
        plain_dot(normed, w_value)
        .astype(jnp.bfloat16)
        .reshape(batch_count, segment_len, value_width)
    )
    gate_pre = plain_dot(normed, w_gate)
    rate_pre = plain_dot(normed, w_rate)
    behind = passed_along(
        (
            query_pre[:, segment_len - conv_lead :],
            key_pre[:, segment_len - conv_lead :],
            value_pre[:, segment_len - conv_lead :],
        ),
        "seq",
        1,
    )
    query_ext = jnp.concatenate([behind[0], query_pre], axis=1).astype(jnp.float32)
    key_ext = jnp.concatenate([behind[1], key_pre], axis=1).astype(jnp.float32)
    value_ext = jnp.concatenate([behind[2], value_pre], axis=1).astype(jnp.float32)
    prepared, prep_back = jax.vjp(
        prepare,
        query_ext,
        key_ext,
        value_ext,
        rate_pre.reshape(batch_count, segment_len, -1),
        conv_weight,
        decay_log,
        decay_bias,
    )
    queries, key_rows, values, beta_rows, decays = prepared
    queries = round_trip(queries)
    key_rows = round_trip(key_rows)
    values = round_trip(values)
    head_count = decay_log.shape[0]
    group_count = segment_len // GROUP

    def by_group(rows):
        moved = jnp.moveaxis(rows, 2, 1)
        return moved.reshape((batch_count, head_count, group_count, GROUP) + rows.shape[3:])

    def by_token(rows):
        joined = rows.reshape((batch_count, head_count, segment_len) + rows.shape[4:])
        return jnp.moveaxis(joined, 1, 2)

    (step_map, step_offset, read_map, read_offset), maps_back = jax.vjp(
        group_maps,
        by_group(queries),
        by_group(key_rows),
        by_group(values),
        by_group(beta_rows),
        by_group(decays),
    )
    maps = [step_map[:, :, g] for g in range(group_count)]
    offsets = [step_offset[:, :, g] for g in range(group_count)]
    mapping = maps[0]
    offset = offsets[0]
    for g in range(1, group_count):
        mapping = mid_dot(maps[g], mapping, "shij,shjk->shik")
        offset = mid_dot(maps[g], offset, "shij,shjk->shik") + offsets[g]
    entering = hop_sum(offset, 1)
    for hop_index in range(lax.axis_size("seq") - 2):
        entering = hop_sum(mid_dot(mapping, entering, "shij,shjk->shik") + offset, 1)
    states = [entering]
    for g in range(group_count - 1):
        states.append(mid_dot(maps[g], states[g], "shij,shjk->shik") + offsets[g])
    states = jnp.stack(states, axis=2)
    mixture = mid_dot(read_map, states, "shgtk,shgkv->shgtv") + read_offset
    gated_full, gate_back = jax.vjp(
        gate_output,
        by_token(mixture),
        gate_pre.reshape(batch_count, segment_len, value_width),
        out_gain,
    )
    gated = gated_full.reshape(row_count, value_width).astype(jnp.bfloat16)
    hidden = tokens + plain_dot(gated, w_output)
    normed_two_full, norm_two_back = jax.vjp(rms_scale, hidden, ffn_gain)
    normed_two = normed_two_full.astype(jnp.bfloat16)
    gate_vals = plain_dot(normed_two, w_ffgate)
    up_vals = plain_dot(normed_two, w_ffup)
    product_full, swiglu_back = jax.vjp(swiglu_product, gate_vals, up_vals)
    product = product_full.astype(jnp.bfloat16)
    outputs = (hidden + plain_dot(product, w_ffdown)).astype(jnp.bfloat16).reshape(inputs.shape)
    cotangent = upstream.reshape(row_count, model_width)
    product_grad = back_dot(cotangent, w_ffdown)
    grad_down = weight_dot(product, cotangent)
    gate_grad_full, up_grad_full = swiglu_back(product_grad)
    gate_grad = gate_grad_full.astype(jnp.bfloat16)
    up_grad = up_grad_full.astype(jnp.bfloat16)
    normed_two_grad = back_dot(gate_grad, w_ffgate) + back_dot(up_grad, w_ffup)
    grad_ffgate = weight_dot(normed_two, gate_grad)
    grad_ffup = weight_dot(normed_two, up_grad)
    hidden_part, ffn_gain_grad = norm_two_back(normed_two_grad)
    hidden_grad = cotangent.astype(jnp.float32) + hidden_part
    branch_grad = hidden_grad.astype(jnp.bfloat16)
    gated_grad = back_dot(branch_grad, w_output)
    grad_output = weight_dot(gated, branch_grad)
    mixture_grad_rows, gate_pre_grad, out_gain_grad = gate_back(
        gated_grad.reshape(batch_count, segment_len, value_width)
    )
    mixture_grad = by_group(mixture_grad_rows)
    read_grads = mid_dot(read_map, mixture_grad, "shgtk,shgtv->shgkv")
    reads = [read_grads[:, :, g] for g in range(group_count)]
    local_term = reads[group_count - 1]
    for g in range(group_count - 2, -1, -1):
        local_term = mid_dot(maps[g], local_term, "shji,shjk->shik") + reads[g]
    leaving = hop_sum(local_term, -1)
    for hop_index in range(lax.axis_size("seq") - 2):
        leaving = hop_sum(mid_dot(mapping, leaving, "shji,shjk->shik") + local_term, -1)
    after = [leaving]
    for g in range(group_count - 1, 0, -1):
        after.append(mid_dot(maps[g], after[-1], "shji,shjk->shik") + reads[g])
    after = jnp.stack(after[::-1], axis=2)
    query_grad, key_grad, value_grad, beta_grad, decay_grad = maps_back(
        (
            mid_dot(after, states, "shgkv,shgjv->shgkj"),
            after,
            mid_dot(mixture_grad, states, "shgtv,shgkv->shgtk"),
            mixture_grad,
        )
    )
    ext_grads = prep_back(
        (
            by_token(round_trip(query_grad)),
            by_token(round_trip(key_grad)),
            by_token(round_trip(value_grad)),
            by_token(beta_grad),
            by_token(decay_grad),
        )
    )
    (
        query_ext_grad,
        key_ext_grad,
        value_ext_grad,
        rate_grad_full,
        conv_grad,
        decay_log_grad,
        decay_bias_grad,
    ) = ext_grads
    returned = (
        passed_along(query_ext_grad[:, :conv_lead].astype(jnp.bfloat16), "seq", -1).astype(
            jnp.float32
        ),
        passed_along(key_ext_grad[:, :conv_lead].astype(jnp.bfloat16), "seq", -1).astype(
            jnp.float32
        ),
        passed_along(value_ext_grad[:, :conv_lead].astype(jnp.bfloat16), "seq", -1).astype(
            jnp.float32
        ),
    )

    def settle(ext_grad, incoming, channels):
        own_rows = ext_grad[:, conv_lead:]
        own_rows = jnp.concatenate(
            [
                own_rows[:, : segment_len - conv_lead],
                own_rows[:, segment_len - conv_lead :] + incoming,
            ],
            axis=1,
        )
        return own_rows.reshape(row_count, channels).astype(jnp.bfloat16)

    query_pre_grad = settle(query_ext_grad, returned[0], key_width)
    key_pre_grad = settle(key_ext_grad, returned[1], key_width)
    value_pre_grad = settle(value_ext_grad, returned[2], value_width)
    gate_pre_rounded = gate_pre_grad.reshape(row_count, value_width).astype(jnp.bfloat16)
    rate_grad = rate_grad_full.reshape(row_count, -1).astype(jnp.bfloat16)
    normed_grad = (
        back_dot(query_pre_grad, w_query)
        + back_dot(key_pre_grad, w_key)
        + back_dot(value_pre_grad, w_value)
        + back_dot(gate_pre_rounded, w_gate)
        + back_dot(rate_grad, w_rate)
    )
    grad_query = weight_dot(normed, query_pre_grad)
    grad_key = weight_dot(normed, key_pre_grad)
    grad_value = weight_dot(normed, value_pre_grad)
    grad_gate = weight_dot(normed, gate_pre_rounded)
    grad_rate = weight_dot(normed, rate_grad)
    token_part, norm_gain_grad = norm_back(normed_grad)
    input_grad = (hidden_grad + token_part).reshape(inputs.shape)
    summed = column_sums(
        tuple(
            row_sum(grad)
            for grad in (
                grad_query,
                grad_key,
                grad_value,
                grad_gate,
                grad_rate,
                grad_output,
                grad_ffgate,
                grad_ffup,
                grad_down,
            )
        )
    )
    small_grads = (
        norm_gain_grad,
        conv_grad,
        decay_log_grad,
        decay_bias_grad,
        out_gain_grad,
        ffn_gain_grad,
    )
    joined = lax.psum(jnp.concatenate([grad.reshape(-1) for grad in small_grads]), ("dp", "seq"))
    small_sums = []
    start = 0
    for grad in small_grads:
        small_sums.append(joined[start : start + grad.size].reshape(grad.shape))
        start = start + grad.size
    return (
        outputs,
        input_grad,
        small_sums[0],
        summed[0],
        summed[1],
        summed[2],
        summed[3],
        summed[4],
        small_sums[1],
        small_sums[2],
        small_sums[3],
        small_sums[4],
        summed[5],
        small_sums[5],
        summed[6],
        summed[7],
        summed[8],
    )


def solution(mesh):
    in_specs = (
        P(None, "dp", "seq", None),
        P(None, "dp", "seq", None),
        P(),
        P("dp", "seq"),
        P("dp", "seq"),
        P("dp", "seq"),
        P("dp", "seq"),
        P("dp", "seq"),
        P(),
        P(),
        P(),
        P(),
        P("dp", "seq"),
        P(),
        P("dp", "seq"),
        P("dp", "seq"),
        P("dp", "seq"),
    )
    out_specs = (
        P(None, "dp", "seq", None),
        P(None, "dp", "seq", None),
        P(),
        P("dp", "seq"),
        P("dp", "seq"),
        P("dp", "seq"),
        P("dp", "seq"),
        P("dp", "seq"),
        P(),
        P(),
        P(),
        P(),
        P("dp", "seq"),
        P(),
        P("dp", "seq"),
        P("dp", "seq"),
        P("dp", "seq"),
    )
    return jax.shard_map(shards, mesh=mesh, in_specs=in_specs, out_specs=out_specs, check_vma=False)
```
